256 devices in a mesh: outer: 32 (over z, x_lo, core), inner: 8 (over x_hi, y).
Axes of the slice: x: 4 (x_hi: 2, x_lo: 2; x = x_hi * 2 + x_lo), y: 4, z: 8, core: 2. Of those that a mesh axis runs over, the one named last changes fastest.
Arguments:
- queries: bfloat16 [65536, 4096], P(('outer', 'inner')), may hold values from -136 to 136
- keys: bfloat16 [65536, 512], P(('outer', 'inner')), may hold values from -6 to 6
- values: bfloat16 [65536, 512], P(('outer', 'inner')), may hold values from -6 to 6
- segment: int32 [65536], P(('outer', 'inner')), may hold values from 0 to 31, never falling along the last dimension, each value on 1 to 4096 neighbouring positions
- signs: int32 [128], replicated, may hold values from 0 to 1
Outputs:
- attended: bfloat16 [65536, 4096], P(('outer', 'inner'))
The draws below stay inside these ranges and needn't reach their ends.
Inputs may be any that keep to these rules, and one draw needn't show every extreme that they name: `segment`: document numbers never fall along the sequence; each document holds 1 to 4096 tokens, and one holds exactly that many.
All inputs are finite; a program needn't handle non-finite values.
Results may differ from the reference program's by a relative error of at most 0.0057.
Values may be sent and summed in bfloat16 or wider, within the bound.
A program may use at most 192 MiB of HBM per device.

```python
import math
import jax
import jax.numpy as jnp
import numpy as np
from jax import lax

QUERY_HEADS = 32
KEY_VALUE_HEADS = 4
HEAD_DIMENSION = 128
TOK_DEV = 256
SEQUENCE_TOKENS = 65536
DOCS = 32
N_INNER = 8


def draw_queries(key, part):
    key = jax.random.fold_in(key, 11)
    first = jax.random.fold_in(key, 0)
    base = jnp.clip(jax.random.normal(first, (SEQUENCE_TOKENS, QUERY_HEADS * HEAD_DIMENSION), jnp.float32), -6.0, 6.0)
    return base.astype(jnp.bfloat16)


def touch_ends(entries, stream_key, least, largest):
    longest = entries.shape.index(max(entries.shape))
    spots = []
    for shift in (0, 1):
        where = [jax.random.randint(jax.random.fold_in(stream_key, axis), (), 0, length) for axis, length in enumerate(entries.shape)]
        where[longest] = (where[longest] + shift) % entries.shape[longest]
        spots.append(tuple(where))
    return entries.at[spots[0]].set(least).at[spots[1]].set(largest)


def shard_levels(own_key, shape, shards, low, top_value):
    level, own = 1.0, jax.random.fold_in(own_key, 6)
    for dim, shards_of in shards:
        steps = jnp.exp(jax.random.uniform(jax.random.fold_in(own, dim), (shards_of,), jnp.float32, low / len(shards), top_value / len(shards)))
        level = level * jnp.repeat(steps, shape[dim] // shards_of).reshape([-1 if axis == dim else 1 for axis in range(len(shape))])
    return level


def length_profile(count, total, limit, skew):
    weights = [(1 << 20) // math.isqrt(rank ** skew) + 1 for rank in range(2, count + 1)]
    rest, given = total - limit - (count - 1), [1] * (count - 1)
    while rest > 0:
        free = [i for i in range(count - 1) if given[i] < limit]
        mass, budget = sum([weights[i] for i in free]), rest
        for i in free:
            addition = min(limit - given[i], max(1, budget * weights[i] // mass), rest)
            given[i] = given[i] + addition
            rest = rest - addition
    return np.array([limit] + given)


def ragged(key, amount, total, bound, slope):
    if amount == 2:
        one = jax.random.randint(key, (), max(1, total - bound), min(bound, total - 1) + 1)
        return jnp.stack([one, total - one])
    sizes = jnp.asarray(length_profile(amount, total, bound, slope), jnp.int32)
    twos = (amount - 1) // 2
    donor, taker = sizes[1:1 + 2 * twos:2], sizes[2:2 + 2 * twos:2]
    slack = jnp.minimum(donor - 1, bound - taker)
    shifted = jax.random.randint(jax.random.fold_in(key, 1), (twos,), 0, 1 << 20) % (slack + 1)
    sizes = sizes.at[1:1 + 2 * twos:2].set(donor - shifted).at[2:2 + 2 * twos:2].set(taker + shifted)
    return sizes[jax.random.permutation(jax.random.fold_in(key, 2), amount)]


def normal_values(key, shape, scale, limit, shards=(), kind=jnp.bfloat16):
    array = jax.random.normal(key, shape, jnp.float32) * scale
    if len(shards) > 0:
        array = shard_levels(key, shape, shards, -0.22, 0.18) * array
    return jnp.clip(array, min=-limit, max=limit).astype(kind)


def setup_inputs(seed: int = 0) -> dict:
    streams_of = jax.random.split(jax.random.key(seed), 6)
    queries = draw_queries(jax.random.fold_in(streams_of[5], 71), 0)
    keys = normal_values(streams_of[1], (SEQUENCE_TOKENS, KEY_VALUE_HEADS * HEAD_DIMENSION), 1.0, 6.0, ((0, 256),))
    values = normal_values(streams_of[2], (SEQUENCE_TOKENS, KEY_VALUE_HEADS * HEAD_DIMENSION), 1.0, 6.0, ((0, 256),))
    segment = jnp.searchsorted(jnp.cumsum(ragged(streams_of[3], DOCS, SEQUENCE_TOKENS, 16 * TOK_DEV, 0)), jnp.arange(SEQUENCE_TOKENS), side="right").astype(jnp.int32)
    signs = touch_ends(jax.random.randint(streams_of[4], (HEAD_DIMENSION,), 0, 2), jax.random.fold_in(streams_of[4], 1), 0, 1).astype(jnp.int32)
    return {"queries": queries, "keys": keys, "values": values, "segment": segment, "signs": signs}


def hadamard_table(order):
    table = np.ones((1, 1))
    while table.shape[0] < order:
        upper = np.concatenate([table, table], axis=1)
        lower = np.concatenate([table, -table], axis=1)
        table = np.concatenate([upper, lower], axis=0)
    return table / np.sqrt(order)

def rotate(values, signs):
    heads = values.shape[1] // HEAD_DIMENSION
    flips = (1 - 2 * signs).astype(jnp.float32)
    scaled = values.astype(jnp.float32).reshape(-1, heads, HEAD_DIMENSION) * flips
    table = jnp.asarray(hadamard_table(HEAD_DIMENSION), jnp.float32)
    turned = jnp.dot(scaled.reshape(-1, HEAD_DIMENSION), table, precision=lax.Precision.HIGHEST)
    return turned.reshape(values.shape[0], heads * HEAD_DIMENSION).astype(jnp.bfloat16)

def attend(query_row_block, key_row_block, value_row_block, visible):
    token_rows = query_row_block.shape[0]
    sequence_length = key_row_block.shape[0]
    query_group = QUERY_HEADS // KEY_VALUE_HEADS
    query_float = query_row_block.astype(jnp.float32).reshape(token_rows, KEY_VALUE_HEADS, query_group, HEAD_DIMENSION)
    key_float = key_row_block.astype(jnp.float32).reshape(sequence_length, KEY_VALUE_HEADS, HEAD_DIMENSION)
    scores = jnp.einsum('bhgd,lhd->hgbl', query_float, key_float) / jnp.sqrt(jnp.float32(HEAD_DIMENSION))
    scores = jnp.where(visible[None, None], scores, jnp.float32(-1e+30))
    top = lax.optimization_barrier(jnp.max(scores, axis=-1, keepdims=True))
    expo = jnp.exp(scores - top)
    total = lax.optimization_barrier(jnp.sum(expo, axis=-1, keepdims=True))
    weights = (expo / total).astype(jnp.bfloat16)
    value_float = value_row_block.astype(jnp.float32).reshape(sequence_length, KEY_VALUE_HEADS, HEAD_DIMENSION)
    mixed = jnp.einsum('hgbl,lhd->bhgd', weights.astype(jnp.float32), value_float)
    return mixed.reshape(token_rows, QUERY_HEADS * HEAD_DIMENSION).astype(jnp.bfloat16)

def reference(queries, keys, values, segment, signs):
    rotated = rotate(values, signs)
    blocks = SEQUENCE_TOKENS // TOK_DEV
    offsets = [0, 1, N_INNER, N_INNER + 1]
    rows_idx = jnp.arange(TOK_DEV, dtype=jnp.int32)

    def one_block(index):
        start = (index * TOK_DEV).astype(jnp.int32)
        query_row_block = lax.dynamic_slice_in_dim(queries, start, TOK_DEV, 0)
        query_seg = lax.dynamic_slice_in_dim(segment, start, TOK_DEV, 0)
        key_list, value_list, masks = ([], [], [])
        for offset in offsets:
            source = index - offset
            begin = (jnp.maximum(source, 0) * TOK_DEV).astype(jnp.int32)
            key_list.append(lax.dynamic_slice_in_dim(keys, begin, TOK_DEV, 0))
            value_list.append(lax.dynamic_slice_in_dim(rotated, begin, TOK_DEV, 0))
            key_seg = lax.dynamic_slice_in_dim(segment, begin, TOK_DEV, 0)
            allowed = (query_seg[:, None] == key_seg[None, :]) & (source >= 0)
            if offset == 0:
                allowed = allowed & (rows_idx[:, None] >= rows_idx[None, :])
            masks.append(allowed)
        return attend(query_row_block, jnp.concatenate(key_list, 0), jnp.concatenate(value_list, 0), jnp.concatenate(masks, 1))
    result = lax.map(one_block, jnp.arange(blocks, dtype=jnp.int32))
    return result.reshape(SEQUENCE_TOKENS, QUERY_HEADS * HEAD_DIMENSION)
```

```python
import functools
import math

import jax
import jax.numpy as jnp
from jax import lax
from jax.experimental import pallas as pl
from jax.experimental.pallas import tpu as pltpu
from jax.sharding import PartitionSpec as P

MESH = pl.DeviceIdType.MESH
BLOCK = 256
HEAD = 128
KV = 4
GROUP = 8
ROWS = 2 * BLOCK + 16
NEG = -1e30
NO_DOC = 127
SCALE = math.log2(math.e) / math.sqrt(HEAD)
ROW_BY_ROW = (((1,), (1,)), ((), ()))
BF16 = jnp.bfloat16
F32 = jnp.float32


def hadamard_signs():
    left = lax.broadcasted_iota(jnp.int32, (HEAD, HEAD), 0)
    right = lax.broadcasted_iota(jnp.int32, (HEAD, HEAD), 1)
    both = left & right
    both = both ^ (both >> 4)
    both = both ^ (both >> 2)
    both = both ^ (both >> 1)
    return (1 - 2 * (both & 1)).astype(F32).astype(BF16)


def documents(packet_rows):
    parts = []
    for half in range(2):
        row = packet_rows[8 * half : 8 * half + 1, :].astype(F32)
        ids = lax.broadcasted_iota(jnp.int32, (HEAD, HEAD), 0).astype(F32)
        parts.append(jnp.where(row == ids, F32(1), F32(0)).T)
    return jnp.concatenate(parts, axis=0)


def kernel(
    n_outer, n_inner, q_hbm, k_hbm, v_hbm, seg_ref, signs_ref, o_hbm,
    q, raw, packs, out, top, acc, bias, away, docs,
    q_sem, k_sem, v_sem, o_sem, send, recv,
):
    me = lax.axis_index("outer") * n_inner + lax.axis_index("inner")
    count = n_outer * n_inner

    def device(index):
        return {"outer": lax.div(index, n_inner), "inner": lax.rem(index, n_inner)}

    offsets = (1, n_inner)
    barrier = pltpu.get_barrier_semaphore()
    for offset in offsets:
        @pl.when(me >= offset)
        def _():
            pl.semaphore_signal(barrier, inc=1, device_id=device(me - offset), device_id_type=MESH)

    def columns(h):
        return pl.ds(h * HEAD, HEAD)

    k_in = [pltpu.make_async_copy(k_hbm.at[:, columns(h)], packs.at[0, h, pl.ds(0, BLOCK)], k_sem.at[h]) for h in range(KV)]
    v_in = [pltpu.make_async_copy(v_hbm.at[:, columns(h)], raw.at[h], v_sem.at[h]) for h in range(KV)]
    wide = GROUP * HEAD
    q_in = [pltpu.make_async_copy(q_hbm.at[:, pl.ds(g * wide, wide)], q.at[g], q_sem.at[g]) for g in range(KV)]
    for copy in v_in + k_in + q_in:
        copy.start()

    seg = seg_ref[...].astype(F32)
    lower = lax.broadcasted_iota(jnp.int32, (16, HEAD), 0) < 8
    own_rows = jnp.where(lower, seg[:, :HEAD], seg[:, HEAD:]).astype(BF16)
    flips = (1 - 2 * signs_ref[...]).astype(F32)
    table = hadamard_signs()

    for h in range(KV):
        v_in[h].wait()
        turned = jnp.dot((raw[h].astype(F32) * flips).astype(BF16), table, preferred_element_type=F32)
        packs[0, h, BLOCK : 2 * BLOCK, :] = (turned * F32(1 / math.sqrt(HEAD))).astype(BF16)
        packs[0, h, 2 * BLOCK :, :] = own_rows
        k_in[h].wait()

    for place, offset in ((1, 1), (2, n_inner), (3, n_inner + 1)):
        @pl.when(me < offset)
        def _():
            for h in range(KV):
                packs[place, h, : 2 * BLOCK, :] = jnp.zeros((2 * BLOCK, HEAD), BF16)
                packs[place, h, 2 * BLOCK :, :] = jnp.full((16, HEAD), NO_DOC, BF16)

    def carry(source, place, h, offset):
        return pltpu.make_async_remote_copy(
            src_ref=packs.at[source, h], dst_ref=packs.at[place, h],
            send_sem=send.at[place - 1, h], recv_sem=recv.at[place - 1, h],
            device_id=device(me + offset), device_id_type=MESH,
        )

    near = [carry(0, 1, h, 1) for h in range(KV)]
    hop = [carry(0, 2, h, n_inner) for h in range(KV)]
    far = [carry(1, 3, h, n_inner) for h in range(KV)]
    has_near, has_hop, has_far = me >= 1, me >= n_inner, me >= n_inner + 1
    to_near, to_hop = me + 1 < count, me + n_inner < count
    to_far = has_near & to_hop

    pl.when(to_hop)(lambda: pl.semaphore_wait(barrier, 2))
    pl.when(to_near & (me + n_inner >= count))(lambda: pl.semaphore_wait(barrier, 1))
    for h in range(KV):
        pl.when(to_near)(near[h].start)
        pl.when(to_hop)(hop[h].start)

    own = documents(packs[0, 0, 2 * BLOCK :, :])
    same = lax.dot_general(own.astype(BF16), own.astype(BF16), ROW_BY_ROW, preferred_element_type=F32)
    row = lax.broadcasted_iota(jnp.int32, (BLOCK, BLOCK), 0)
    column = lax.broadcasted_iota(jnp.int32, (BLOCK, BLOCK), 1)
    bias[...] = jnp.where((same > 0.5) & (row >= column), F32(0), F32(NEG))
    away[...] = jnp.where(own > 0.5, F32(0), F32(NEG)).astype(BF16)
    ones = jnp.ones((BLOCK, HEAD), BF16)

    def values_of(place, g):
        return jnp.concatenate([packs[place, g, BLOCK : 2 * BLOCK, :], ones], axis=1)

    for g in range(KV):
        q_in[g].wait()
        for j in range(GROUP):
            scores = lax.dot_general(
                q[g, :, j * HEAD : (j + 1) * HEAD], packs[0, g, :BLOCK, :], ROW_BY_ROW, preferred_element_type=F32
            ) + bias[...]
            peak = jnp.max(scores, axis=1, keepdims=True)
            weights = jnp.exp2((scores - peak) * SCALE).astype(BF16)
            top[g * GROUP + j] = jnp.broadcast_to(peak, (BLOCK, HEAD))
            acc[g * GROUP + j] = jnp.dot(weights, values_of(0, g), preferred_element_type=F32)

    def arrive(h):
        pl.when(has_near)(near[h].wait_recv)
        pl.when(to_far)(far[h].start)

    def attend(g):
        pl.when(has_hop)(hop[g].wait_recv)
        pl.when(has_far)(far[g].wait_recv)
        if g == 0:
            for place in (1, 2, 3):
                docs[place - 1] = documents(packs[place, 0, 2 * BLOCK :, :]).astype(BF16)
        for j in range(GROUP):
            query = jnp.concatenate([q[g, :, j * HEAD : (j + 1) * HEAD], away[...]], axis=1)
            scores = []
            for place in (1, 2, 3):
                key = jnp.concatenate([packs[place, g, :BLOCK, :], docs[place - 1]], axis=1)
                scores.append(lax.dot_general(query, key, ROW_BY_ROW, preferred_element_type=F32))
            before = top[g * GROUP + j][:, :1]
            peak = jnp.max(functools.reduce(jnp.maximum, scores), axis=1, keepdims=True)
            peak = jnp.maximum(peak, before)
            total = acc[g * GROUP + j] * jnp.exp2((before - peak) * SCALE)
            for place in (1, 2, 3):
                weights = jnp.exp2((scores[place - 1] - peak) * SCALE).astype(BF16)
                total = total + jnp.dot(weights, values_of(place, g), preferred_element_type=F32)
            out[g, :, j * HEAD : (j + 1) * HEAD] = (total[:, :HEAD] / total[:, HEAD:]).astype(BF16)
        copy = pltpu.make_async_copy(out.at[g], o_hbm.at[:, pl.ds(g * wide, wide)], o_sem.at[g])
        copy.start()
        return copy

    arrive(0)
    arrive(1)
    outs = [attend(0)]
    arrive(2)
    outs.append(attend(1))
    arrive(3)
    outs.append(attend(2))
    outs.append(attend(3))
    for h in range(KV):
        pl.when(to_near)(near[h].wait_send)
        pl.when(to_hop)(hop[h].wait_send)
        pl.when(to_far)(far[h].wait_send)
        outs[h].wait()


def solution(mesh):
    n_outer, n_inner = mesh.shape["outer"], mesh.shape["inner"]

    def on_device(queries, keys, values, segment, signs):
        anywhere = pl.BlockSpec(memory_space=pl.ANY)
        here = pl.BlockSpec(memory_space=pltpu.VMEM)
        return pl.pallas_call(
            functools.partial(kernel, n_outer, n_inner),
            out_shape=jax.ShapeDtypeStruct(queries.shape, BF16),
            in_specs=[anywhere, anywhere, anywhere, here, here],
            out_specs=anywhere,
            scratch_shapes=[
                pltpu.VMEM((KV, BLOCK, GROUP * HEAD), BF16),
                pltpu.VMEM((KV, BLOCK, HEAD), BF16),
                pltpu.VMEM((4, KV, ROWS, HEAD), BF16),
                pltpu.VMEM((KV, BLOCK, GROUP * HEAD), BF16),
                pltpu.VMEM((KV * GROUP, BLOCK, HEAD), F32),
                pltpu.VMEM((KV * GROUP, BLOCK, 2 * HEAD), F32),
                pltpu.VMEM((BLOCK, BLOCK), F32),
                pltpu.VMEM((BLOCK, HEAD), BF16),
                pltpu.VMEM((3, BLOCK, HEAD), BF16),
                pltpu.SemaphoreType.DMA((KV,)),
                pltpu.SemaphoreType.DMA((KV,)),
                pltpu.SemaphoreType.DMA((KV,)),
                pltpu.SemaphoreType.DMA((KV,)),
                pltpu.SemaphoreType.DMA((3, KV)),
                pltpu.SemaphoreType.DMA((3, KV)),
            ],
            compiler_params=pltpu.CompilerParams(
                collective_id=0, has_side_effects=True, vmem_limit_bytes=62 * 2**20
            ),
        )(queries, keys, values, segment.reshape(1, BLOCK), signs.reshape(1, HEAD))

    placed = (
        P(("outer", "inner"), None),
        P(("outer", "inner"), None),
        P(("outer", "inner"), None),
        P(("outer", "inner")),
        P(),
    )
    return jax.shard_map(
        on_device, mesh=mesh, in_specs=placed, out_specs=P(("outer", "inner"), None), check_vma=False
    )
```

```python
import functools
import math

import jax
import jax.numpy as jnp
from jax import lax
from jax.experimental import pallas as pl
from jax.experimental.pallas import tpu as pltpu
from jax.sharding import PartitionSpec as P

MESH = pl.DeviceIdType.MESH
BLOCK = 256
HEAD = 128
KV = 4
GROUP = 8
ROWS = 2 * BLOCK + 16
NEG = -1e30
NO_DOC = 127
SCALE = math.log2(math.e) / math.sqrt(HEAD)
ROW_BY_ROW = (((1,), (1,)), ((), ()))
BF16 = jnp.bfloat16
F32 = jnp.float32


def hadamard_signs():
    left = lax.broadcasted_iota(jnp.int32, (HEAD, HEAD), 0)
    right = lax.broadcasted_iota(jnp.int32, (HEAD, HEAD), 1)
    both = left & right
    both = both ^ (both >> 4)
    both = both ^ (both >> 2)
    both = both ^ (both >> 1)
    return (1 - 2 * (both & 1)).astype(F32).astype(BF16)


def documents(packet_rows):
    parts = []
    for half in range(2):
        row = packet_rows[8 * half : 8 * half + 1, :].astype(F32)
        ids = lax.broadcasted_iota(jnp.int32, (HEAD, HEAD), 0).astype(F32)
        parts.append(jnp.where(row == ids, F32(1), F32(0)).T)
    return jnp.concatenate(parts, axis=0)


def twice(block):
    return jnp.concatenate([block, block], axis=1)


def row_peak(first, second):
    both = jnp.maximum(first, second)
    both = jnp.maximum(both[:, :HEAD], both[:, HEAD:])
    return jnp.broadcast_to(jnp.max(both, axis=1, keepdims=True), (BLOCK, HEAD))


def kernel(
    n_outer, n_inner, q_hbm, k_hbm, v_hbm, seg_ref, signs_ref, o_hbm,
    q, raw, packs, out, top, acc, bias, away, docs,
    q_sem, k_sem, v_sem, o_sem, send, recv,
):
    count = n_outer * n_inner

    def device(index):
        return {"outer": lax.div(index, n_inner), "inner": lax.rem(index, n_inner)}

    outer, inner = lax.axis_index("outer"), lax.axis_index("inner")
    me = outer * n_inner + inner
    even = lax.rem(outer, 2) == 0
    odd = lax.rem(outer, 2) == 1
    half = n_inner // 2
    turn = inner == half - 1
    wraps = odd & turn
    late = (inner == half - 1) | (inner == n_inner - 1)
    early = (inner == half - 2) | (inner == n_inner - 2)

    has_near = me >= 1
    has_hop = (me >= n_inner) | (me == half - 1)
    has_far = me >= n_inner + 1
    to_near = (me + 1 < count) & jnp.logical_not(wraps)
    to_hop = (me + n_inner < count) | (me == count - half - 1)
    to_back = even & turn
    to_far = has_near & (me + n_inner < count)
    to_far_late = to_far & jnp.logical_not(odd & late)
    to_side = even & early & (me >= n_inner)

    hop_index = lax.rem(me + n_inner, count)
    back_index = lax.rem(me - n_inner + 1 + count, count)
    hop_source = lax.rem(me - n_inner + count, count)
    near_source = jnp.where(odd & (inner == half), lax.rem(me + n_inner - 1, count), me - 1)

    barrier = pltpu.get_barrier_semaphore()
    for comes, source in ((has_near, near_source), (has_hop, hop_source)):
        @pl.when(comes)
        def _():
            pl.semaphore_signal(barrier, inc=1, device_id=device(source), device_id_type=MESH)

    def columns(h):
        return pl.ds(h * HEAD, HEAD)

    k_in = [pltpu.make_async_copy(k_hbm.at[:, columns(h)], packs.at[0, h, pl.ds(0, BLOCK)], k_sem.at[h]) for h in range(KV)]
    v_in = [pltpu.make_async_copy(v_hbm.at[:, columns(h)], raw.at[h], v_sem.at[h]) for h in range(KV)]
    wide = GROUP * HEAD
    q_in = [pltpu.make_async_copy(q_hbm.at[:, pl.ds(g * wide, wide)], q.at[g], q_sem.at[g]) for g in range(KV)]
    for copy in v_in + k_in + q_in:
        copy.start()

    seg = seg_ref[...].astype(F32)
    lower = lax.broadcasted_iota(jnp.int32, (16, HEAD), 0) < 8
    own_rows = jnp.where(lower, seg[:, :HEAD], seg[:, HEAD:]).astype(BF16)
    flips = (1 - 2 * signs_ref[...]).astype(F32)
    table = hadamard_signs()

    for h in range(KV):
        v_in[h].wait()
        turned = jnp.dot((raw[h].astype(F32) * flips).astype(BF16), table, preferred_element_type=F32)
        packs[0, h, BLOCK : 2 * BLOCK, :] = (turned * F32(1 / math.sqrt(HEAD))).astype(BF16)
        packs[0, h, 2 * BLOCK :, :] = own_rows
        k_in[h].wait()

    for place, comes in ((1, has_near), (2, has_hop), (3, has_far)):
        @pl.when(jnp.logical_not(comes))
        def _():
            for h in range(KV):
                packs[place, h, : 2 * BLOCK, :] = jnp.zeros((2 * BLOCK, HEAD), BF16)
                packs[place, h, 2 * BLOCK :, :] = jnp.full((16, HEAD), NO_DOC, BF16)

    def carry(source, place, h, index, sent):
        return pltpu.make_async_remote_copy(
            src_ref=packs.at[source, h], dst_ref=packs.at[place, h],
            send_sem=send.at[sent, h], recv_sem=recv.at[place - 1, h],
            device_id=device(index), device_id_type=MESH,
        )

    near = [carry(0, 1, h, me + 1, 0) for h in range(KV)]
    hop = [carry(0, 2, h, hop_index, 1) for h in range(KV)]
    far = [carry(1, 3, h, me + n_inner, 2) for h in range(KV)]
    back = [carry(2, 1, h, back_index, 3) for h in range(KV)]
    side = [carry(2, 3, h, me + 1, 3) for h in range(KV)]

    peers = to_near.astype(jnp.int32) + to_hop.astype(jnp.int32) + to_back.astype(jnp.int32)
    for number in (1, 2, 3):
        @pl.when(peers == number)
        def _():
            pl.semaphore_wait(barrier, number)
    last = inner == n_inner - 1
    first_near = odd | last
    paced_near = jnp.logical_not(first_near | turn)
    for h in range(KV):
        pl.when(to_near & first_near)(near[h].start)
        pl.when(to_hop)(hop[h].start)

    own = documents(packs[0, 0, 2 * BLOCK :, :])
    same = lax.dot_general(own.astype(BF16), own.astype(BF16), ROW_BY_ROW, preferred_element_type=F32)
    row = lax.broadcasted_iota(jnp.int32, (BLOCK, BLOCK), 0)
    column = lax.broadcasted_iota(jnp.int32, (BLOCK, BLOCK), 1)
    bias[...] = jnp.where((same > 0.5) & (row >= column), F32(0), F32(NEG))
    away[...] = jnp.where(own > 0.5, F32(0), F32(NEG)).astype(BF16)
    ones = jnp.ones((BLOCK, HEAD), BF16)

    def values_of(place, g):
        return jnp.concatenate([packs[place, g, BLOCK : 2 * BLOCK, :], ones], axis=1)

    def keys_of(place, g):
        return jnp.concatenate([packs[place, g, :BLOCK, :], docs[place - 1]], axis=1)

    def query_of(g, j):
        return q[g, :, j * HEAD : (j + 1) * HEAD]

    def read_documents(place, exists):
        found = documents(packs[place, 0, 2 * BLOCK :, :])
        none = (lax.broadcasted_iota(jnp.int32, (BLOCK, HEAD), 1) == NO_DOC).astype(F32)
        docs[place - 1] = jnp.where(exists, found, none).astype(BF16)

    def begin(g):
        q_in[g].wait()
        pl.when(to_near & paced_near)(near[g].start)
        pl.when(has_hop)(hop[g].wait_recv)
        pl.when(to_back)(back[g].start)
        pl.when(to_near & even & turn)(near[g].start)
        if g >= KV // 2:
            pl.when(to_side)(side[g].start)
        if g == 0:
            read_documents(2, me >= n_inner)
        for j in range(GROUP):
            query = query_of(g, j)
            wide_query = jnp.concatenate([query, away[...]], axis=1)
            own_scores = lax.dot_general(query, packs[0, g, :BLOCK, :], ROW_BY_ROW, preferred_element_type=F32) + bias[...]
            hop_scores = lax.dot_general(wide_query, keys_of(2, g), ROW_BY_ROW, preferred_element_type=F32)
            peak = row_peak(own_scores, hop_scores)
            total = None
            for place, scores in ((0, own_scores), (2, hop_scores)):
                weights = jnp.exp2((scores - twice(peak)) * SCALE).astype(BF16)
                part = jnp.dot(weights, values_of(place, g), preferred_element_type=F32)
                total = part if total is None else total + part
            top[g * GROUP + j] = peak
            acc[g * GROUP + j] = total

    def arrive(h):
        pl.when(has_near)(near[h].wait_recv)
        pl.when(to_far if h < KV // 2 else to_far_late)(far[h].start)

    def finish(g):
        pl.when(has_far)(far[g].wait_recv)
        if g == 0:
            read_documents(1, me >= 1)
            read_documents(3, me >= n_inner + 1)
        for j in range(GROUP):
            query = jnp.concatenate([query_of(g, j), away[...]], axis=1)
            scores = [
                lax.dot_general(query, keys_of(place, g), ROW_BY_ROW, preferred_element_type=F32) for place in (1, 3)
            ]
            before = top[g * GROUP + j]
            peak = jnp.maximum(row_peak(*scores), before)
            total = acc[g * GROUP + j] * twice(jnp.exp2((before - peak) * SCALE))
            for place, score in zip((1, 3), scores):
                weights = jnp.exp2((score - twice(peak)) * SCALE).astype(BF16)
                total = total + jnp.dot(weights, values_of(place, g), preferred_element_type=F32)
            mass = total[:, HEAD:]
            share = pl.reciprocal(mass, approx=True)
            share = share * (2 - mass * share)
            out[g, :, j * HEAD : (j + 1) * HEAD] = (total[:, :HEAD] * share).astype(BF16)
        copy = pltpu.make_async_copy(out.at[g], o_hbm.at[:, pl.ds(g * wide, wide)], o_sem.at[g])
        copy.start()
        return copy

    for g in range(KV):
        begin(g)
    arrive(0)
    arrive(1)
    outs = [finish(0)]
    arrive(2)
    outs.append(finish(1))
    arrive(3)
    outs += [finish(2), finish(3)]
    for h in range(KV):
        pl.when(to_near)(near[h].wait_send)
        pl.when(to_hop)(hop[h].wait_send)
        pl.when(to_far if h < KV // 2 else to_far_late)(far[h].wait_send)
        pl.when(to_back)(back[h].wait_send)
        if h >= KV // 2:
            pl.when(to_side)(side[h].wait_send)
        outs[h].wait()


def solution(mesh):
    n_outer, n_inner = mesh.shape["outer"], mesh.shape["inner"]

    def on_device(queries, keys, values, segment, signs):
        anywhere = pl.BlockSpec(memory_space=pl.ANY)
        here = pl.BlockSpec(memory_space=pltpu.VMEM)
        return pl.pallas_call(
            functools.partial(kernel, n_outer, n_inner),
            out_shape=pltpu.VMEM(queries.shape, BF16),
            in_specs=[anywhere, anywhere, anywhere, here, here],
            out_specs=anywhere,
            scratch_shapes=[
                pltpu.VMEM((KV, BLOCK, GROUP * HEAD), BF16),
                pltpu.VMEM((KV, BLOCK, HEAD), BF16),
                pltpu.VMEM((4, KV, ROWS, HEAD), BF16),
                pltpu.VMEM((KV, BLOCK, GROUP * HEAD), BF16),
                pltpu.VMEM((KV * GROUP, BLOCK, HEAD), F32),
                pltpu.VMEM((KV * GROUP, BLOCK, 2 * HEAD), F32),
                pltpu.VMEM((BLOCK, BLOCK), F32),
                pltpu.VMEM((BLOCK, HEAD), BF16),
                pltpu.VMEM((3, BLOCK, HEAD), BF16),
                pltpu.SemaphoreType.DMA((KV,)),
                pltpu.SemaphoreType.DMA((KV,)),
                pltpu.SemaphoreType.DMA((KV,)),
                pltpu.SemaphoreType.DMA((KV,)),
                pltpu.SemaphoreType.DMA((4, KV)),
                pltpu.SemaphoreType.DMA((3, KV)),
            ],
            compiler_params=pltpu.CompilerParams(
                collective_id=0, has_side_effects=True, vmem_limit_bytes=60 * 2**20
            ),
        )(queries, keys, values, segment.reshape(1, BLOCK), signs.reshape(1, HEAD))

    placed = (
        P(("outer", "inner"), None),
        P(("outer", "inner"), None),
        P(("outer", "inner"), None),
        P(("outer", "inner")),
        P(),
    )
    return jax.shard_map(
        on_device, mesh=mesh, in_specs=placed, out_specs=P(("outer", "inner"), None), check_vma=False
    )
```

```python
import functools
import math

import jax
import jax.numpy as jnp
from jax import lax
from jax.experimental import pallas as pl
from jax.experimental.pallas import tpu as pltpu
from jax.sharding import PartitionSpec as P

MESH = pl.DeviceIdType.MESH
BLOCK = 256
HEAD = 128
KV = 4
GROUP = 8
ROWS = 2 * BLOCK + 16
NEG = -1e30
NO_DOC = 127
SCALE = math.log2(math.e) / math.sqrt(HEAD)
ROW_BY_ROW = (((1,), (1,)), ((), ()))
BF16 = jnp.bfloat16
F32 = jnp.float32


def hadamard_signs():
    left = lax.broadcasted_iota(jnp.int32, (HEAD, HEAD), 0)
    right = lax.broadcasted_iota(jnp.int32, (HEAD, HEAD), 1)
    both = left & right
    both = both ^ (both >> 4)
    both = both ^ (both >> 2)
    both = both ^ (both >> 1)
    return (1 - 2 * (both & 1)).astype(F32).astype(BF16)


def documents(packet_rows):
    parts = []
    for half in range(2):
        row = packet_rows[8 * half : 8 * half + 1, :].astype(F32)
        ids = lax.broadcasted_iota(jnp.int32, (HEAD, HEAD), 0).astype(F32)
        parts.append(jnp.where(row == ids, F32(1), F32(0)).T)
    return jnp.concatenate(parts, axis=0)


def twice(block):
    return jnp.concatenate([block, block], axis=1)


def row_peak(first, second):
    both = jnp.maximum(first, second)
    both = jnp.maximum(both[:, :HEAD], both[:, HEAD:])
    return jnp.broadcast_to(jnp.max(both, axis=1, keepdims=True), (BLOCK, HEAD))


def kernel(
    n_outer, n_inner, q_hbm, k_hbm, v_hbm, seg_ref, signs_ref, out,
    q, raw, packs, top, acc, bias, away, docs,
    q_sem, k_sem, v_sem, send, recv,
):
    count = n_outer * n_inner

    def device(index):
        return {"outer": lax.div(index, n_inner), "inner": lax.rem(index, n_inner)}

    outer, inner = lax.axis_index("outer"), lax.axis_index("inner")
    me = outer * n_inner + inner
    even = lax.rem(outer, 2) == 0
    odd = lax.rem(outer, 2) == 1
    half = n_inner // 2
    turn = inner == half - 1
    wraps = odd & turn
    late = (inner == half - 1) | (inner == n_inner - 1)
    early = (inner == half - 2) | (inner == n_inner - 2)

    has_near = me >= 1
    has_hop = (me >= n_inner) | (me == half - 1)
    has_far = me >= n_inner + 1
    to_near = (me + 1 < count) & jnp.logical_not(wraps)
    to_hop = (me + n_inner < count) | (me == count - half - 1)
    to_back = even & turn
    to_far = has_near & (me + n_inner < count)
    to_far_late = to_far & jnp.logical_not(odd & late)
    to_side = even & early & (me >= n_inner)
    to_side_first = to_side & (inner == half - 2)
    to_far_first = to_far & jnp.logical_not(odd & turn)

    hop_index = lax.rem(me + n_inner, count)
    back_index = lax.rem(me - n_inner + 1 + count, count)
    hop_source = lax.rem(me - n_inner + count, count)
    near_source = jnp.where(odd & (inner == half), lax.rem(me + n_inner - 1, count), me - 1)

    barrier = pltpu.get_barrier_semaphore()
    for comes, source in ((has_near, near_source), (has_hop, hop_source)):
        @pl.when(comes)
        def _():
            pl.semaphore_signal(barrier, inc=1, device_id=device(source), device_id_type=MESH)

    def columns(h):
        return pl.ds(h * HEAD, HEAD)

    k_in = [pltpu.make_async_copy(k_hbm.at[:, columns(h)], packs.at[0, h, pl.ds(0, BLOCK)], k_sem.at[h]) for h in range(KV)]
    v_in = [pltpu.make_async_copy(v_hbm.at[:, columns(h)], raw.at[h], v_sem.at[h]) for h in range(KV)]
    wide = GROUP * HEAD
    q_in = [pltpu.make_async_copy(q_hbm.at[:, pl.ds(g * wide, wide)], q.at[g], q_sem.at[g]) for g in range(KV)]
    for copy in v_in + k_in + q_in:
        copy.start()

    seg = seg_ref[...].astype(F32)
    lower = lax.broadcasted_iota(jnp.int32, (16, HEAD), 0) < 8
    own_rows = jnp.where(lower, seg[:, :HEAD], seg[:, HEAD:]).astype(BF16)
    flips = (1 - 2 * signs_ref[...]).astype(F32)
    table = hadamard_signs()

    for h in range(KV):
        v_in[h].wait()
        turned = jnp.dot((raw[h].astype(F32) * flips).astype(BF16), table, preferred_element_type=F32)
        packs[0, h, BLOCK : 2 * BLOCK, :] = (turned * F32(1 / math.sqrt(HEAD))).astype(BF16)
        packs[0, h, 2 * BLOCK :, :] = own_rows
        k_in[h].wait()

    for place, comes in ((1, has_near), (2, has_hop), (3, has_far)):
        @pl.when(jnp.logical_not(comes))
        def _():
            for h in range(KV):
                packs[place, h, : 2 * BLOCK, :] = jnp.zeros((2 * BLOCK, HEAD), BF16)
                packs[place, h, 2 * BLOCK :, :] = jnp.full((16, HEAD), NO_DOC, BF16)

    def carry(source, place, h, index, sent):
        return pltpu.make_async_remote_copy(
            src_ref=packs.at[source, h], dst_ref=packs.at[place, h],
            send_sem=send.at[sent, h], recv_sem=recv.at[place - 1, h],
            device_id=device(index), device_id_type=MESH,
        )

    near = [carry(0, 1, h, me + 1, 0) for h in range(KV)]
    hop = [carry(0, 2, h, hop_index, 1) for h in range(KV)]
    far = [carry(1, 3, h, me + n_inner, 2) for h in range(KV)]
    back = [carry(2, 1, h, back_index, 3) for h in range(KV)]
    side = [carry(2, 3, h, me + 1, 3) for h in range(KV)]

    peers = to_near.astype(jnp.int32) + to_hop.astype(jnp.int32) + to_back.astype(jnp.int32)
    for number in (1, 2, 3):
        @pl.when(peers == number)
        def _():
            pl.semaphore_wait(barrier, number)
    last = inner == n_inner - 1
    first_near = odd | last
    paced_near = jnp.logical_not(first_near | turn)
    for h in range(KV):
        pl.when(to_near & first_near)(near[h].start)
        pl.when(to_hop)(hop[h].start)

    own = documents(packs[0, 0, 2 * BLOCK :, :])
    same = lax.dot_general(own.astype(BF16), own.astype(BF16), ROW_BY_ROW, preferred_element_type=F32)
    row = lax.broadcasted_iota(jnp.int32, (BLOCK, BLOCK), 0)
    column = lax.broadcasted_iota(jnp.int32, (BLOCK, BLOCK), 1)
    bias[...] = jnp.where((same > 0.5) & (row >= column), F32(0), F32(NEG))
    away[...] = jnp.where(own > 0.5, F32(0), F32(NEG)).astype(BF16)
    ones = jnp.ones((BLOCK, HEAD), BF16)

    def values_of(place, g):
        return jnp.concatenate([packs[place, g, BLOCK : 2 * BLOCK, :], ones], axis=1)

    def keys_of(place, g):
        return jnp.concatenate([packs[place, g, :BLOCK, :], docs[place - 1]], axis=1)

    def query_of(g, j):
        return q[g, :, j * HEAD : (j + 1) * HEAD]

    def read_documents(place, exists):
        found = documents(packs[place, 0, 2 * BLOCK :, :])
        none = (lax.broadcasted_iota(jnp.int32, (BLOCK, HEAD), 1) == NO_DOC).astype(F32)
        docs[place - 1] = jnp.where(exists, found, none).astype(BF16)

    def begin(g):
        q_in[g].wait()
        pl.when(to_near & paced_near)(near[g].start)
        pl.when(has_hop)(hop[g].wait_recv)
        pl.when(to_back)(back[g].start)
        pl.when(to_near & even & turn)(near[g].start)
        pl.when(to_side_first if g < KV // 2 else to_side)(side[g].start)
        if g == 0:
            read_documents(2, me >= n_inner)
        for j in range(GROUP):
            query = query_of(g, j)
            wide_query = jnp.concatenate([query, away[...]], axis=1)
            own_scores = lax.dot_general(query, packs[0, g, :BLOCK, :], ROW_BY_ROW, preferred_element_type=F32) + bias[...]
            hop_scores = lax.dot_general(wide_query, keys_of(2, g), ROW_BY_ROW, preferred_element_type=F32)
            peak = row_peak(own_scores, hop_scores)
            total = None
            for place, scores in ((0, own_scores), (2, hop_scores)):
                weights = jnp.exp2((scores - twice(peak)) * SCALE).astype(BF16)
                part = jnp.dot(weights, values_of(place, g), preferred_element_type=F32)
                total = part if total is None else total + part
            top[g * GROUP + j] = peak
            acc[g * GROUP + j] = total

    def arrive(h, here):
        pl.when(has_near & here)(near[h].wait_recv)
        pl.when((to_far_first if h < KV // 2 else to_far_late) & here)(far[h].start)

    def merged(place, g, j):
        query = jnp.concatenate([query_of(g, j), away[...]], axis=1)
        scores = lax.dot_general(query, keys_of(place, g), ROW_BY_ROW, preferred_element_type=F32)
        before = top[g * GROUP + j]
        peak = jnp.maximum(row_peak(scores, scores), before)
        weights = jnp.exp2((scores - twice(peak)) * SCALE).astype(BF16)
        part = jnp.dot(weights, values_of(place, g), preferred_element_type=F32)
        return acc[g * GROUP + j] * twice(jnp.exp2((before - peak) * SCALE)) + part, peak

    def extend(g):
        if g == 0:
            read_documents(1, me >= 1)
        for j in range(GROUP):
            acc[g * GROUP + j], top[g * GROUP + j] = merged(1, g, j)

    def finish(g):
        pl.when(has_far)(far[g].wait_recv)
        if g == 0:
            read_documents(3, me >= n_inner + 1)
        for j in range(GROUP):
            total, _ = merged(3, g, j)
            mass = total[:, HEAD:]
            share = pl.reciprocal(mass, approx=True)
            share = share * (2 - mass * share)
            out[:, (g * GROUP + j) * HEAD : (g * GROUP + j + 1) * HEAD] = (total[:, :HEAD] * share).astype(BF16)

    early_near = even & last
    later = jnp.logical_not(early_near)
    for g in range(KV):
        begin(g)
        arrive(g, early_near)
    arrive(0, later)
    extend(0)
    arrive(1, later)
    finish(0)
    extend(1)
    arrive(2, later)
    finish(1)
    extend(2)
    arrive(3, later)
    finish(2)
    extend(3)
    finish(3)
    for h in range(KV):
        pl.when(to_near)(near[h].wait_send)
        pl.when(to_hop)(hop[h].wait_send)
        pl.when(to_far_first if h < KV // 2 else to_far_late)(far[h].wait_send)
        pl.when(to_back)(back[h].wait_send)
        pl.when(to_side_first if h < KV // 2 else to_side)(side[h].wait_send)


def solution(mesh):
    n_outer, n_inner = mesh.shape["outer"], mesh.shape["inner"]

    def on_device(queries, keys, values, segment, signs):
        anywhere = pl.BlockSpec(memory_space=pl.ANY)
        here = pl.BlockSpec(memory_space=pltpu.VMEM)
        return pl.pallas_call(
            functools.partial(kernel, n_outer, n_inner),
            out_shape=pltpu.VMEM(queries.shape, BF16),
            in_specs=[anywhere, anywhere, anywhere, here, here],
            out_specs=here,
            scratch_shapes=[
                pltpu.VMEM((KV, BLOCK, GROUP * HEAD), BF16),
                pltpu.VMEM((KV, BLOCK, HEAD), BF16),
                pltpu.VMEM((4, KV, ROWS, HEAD), BF16),
                pltpu.VMEM((KV * GROUP, BLOCK, HEAD), F32),
                pltpu.VMEM((KV * GROUP, BLOCK, 2 * HEAD), F32),
                pltpu.VMEM((BLOCK, BLOCK), F32),
                pltpu.VMEM((BLOCK, HEAD), BF16),
                pltpu.VMEM((3, BLOCK, HEAD), BF16),
                pltpu.SemaphoreType.DMA((KV,)),
                pltpu.SemaphoreType.DMA((KV,)),
                pltpu.SemaphoreType.DMA((KV,)),
                pltpu.SemaphoreType.DMA((4, KV)),
                pltpu.SemaphoreType.DMA((3, KV)),
            ],
            compiler_params=pltpu.CompilerParams(
                collective_id=0, has_side_effects=True, vmem_limit_bytes=60 * 2**20
            ),
        )(queries, keys, values, segment.reshape(1, BLOCK), signs.reshape(1, HEAD))

    placed = (
        P(("outer", "inner"), None),
        P(("outer", "inner"), None),
        P(("outer", "inner"), None),
        P(("outer", "inner")),
        P(),
    )
    return jax.shard_map(
        on_device, mesh=mesh, in_specs=placed, out_specs=P(("outer", "inner"), None), check_vma=False
    )
```

```python
import functools
import math

import jax
import jax.numpy as jnp
from jax import lax
from jax.experimental import pallas as pl
from jax.experimental.pallas import tpu as pltpu
from jax.sharding import PartitionSpec as P

MESH = pl.DeviceIdType.MESH
BLOCK = 256
HEAD = 128
KV = 4
GROUP = 8
ROWS = 2 * BLOCK + 16
NEG = -1e30
NO_DOC = 127
SCALE = math.log2(math.e) / math.sqrt(HEAD)
ROW_BY_ROW = (((1,), (1,)), ((), ()))
BF16 = jnp.bfloat16
F32 = jnp.float32


def hadamard_signs():
    left = lax.broadcasted_iota(jnp.int32, (HEAD, HEAD), 0)
    right = lax.broadcasted_iota(jnp.int32, (HEAD, HEAD), 1)
    both = left & right
    both = both ^ (both >> 4)
    both = both ^ (both >> 2)
    both = both ^ (both >> 1)
    return (1 - 2 * (both & 1)).astype(F32).astype(BF16)


def documents(packet_rows):
    parts = []
    for half in range(2):
        row = packet_rows[8 * half : 8 * half + 1, :].astype(F32)
        ids = lax.broadcasted_iota(jnp.int32, (HEAD, HEAD), 0).astype(F32)
        parts.append(jnp.where(row == ids, F32(1), F32(0)).T)
    return jnp.concatenate(parts, axis=0)


def twice(block):
    return jnp.concatenate([block, block], axis=1)


def row_peak(first, second):
    both = jnp.maximum(first, second)
    both = jnp.maximum(both[:, :HEAD], both[:, HEAD:])
    return jnp.broadcast_to(jnp.max(both, axis=1, keepdims=True), (BLOCK, HEAD))


def kernel(
    n_outer, n_inner, q_hbm, k_hbm, v_hbm, seg_ref, signs_ref, out,
    q, raw, packs, top, acc, bias, away, docs,
    q_sem, k_sem, v_sem, send, recv,
):
    count = n_outer * n_inner

    def device(index):
        return {"outer": lax.div(index, n_inner), "inner": lax.rem(index, n_inner)}

    outer, inner = lax.axis_index("outer"), lax.axis_index("inner")
    me = outer * n_inner + inner
    even = lax.rem(outer, 2) == 0
    odd = lax.rem(outer, 2) == 1
    half = n_inner // 2
    turn = inner == half - 1
    wraps = odd & turn
    late = (inner == half - 1) | (inner == n_inner - 1)
    early = (inner == half - 2) | (inner == n_inner - 2)

    has_near = me >= 1
    has_hop = (me >= n_inner) | (me == half - 1)
    has_far = me >= n_inner + 1
    to_near = (me + 1 < count) & jnp.logical_not(wraps)
    to_hop = (me + n_inner < count) | (me == count - half - 1)
    to_back = even & turn
    to_far = has_near & (me + n_inner < count)
    to_far_late = to_far & jnp.logical_not(odd & late)
    to_side = even & early & (me >= n_inner)
    to_side_first = to_side & (inner == half - 2)
    to_far_first = to_far & jnp.logical_not(odd & turn)

    hop_index = lax.rem(me + n_inner, count)
    back_index = lax.rem(me - n_inner + 1 + count, count)
    hop_source = lax.rem(me - n_inner + count, count)
    near_source = jnp.where(odd & (inner == half), lax.rem(me + n_inner - 1, count), me - 1)

    barrier = pltpu.get_barrier_semaphore()
    for comes, source in ((has_near, near_source), (has_hop, hop_source)):
        @pl.when(comes)
        def _():
            pl.semaphore_signal(barrier, inc=1, device_id=device(source), device_id_type=MESH)

    def columns(h):
        return pl.ds(h * HEAD, HEAD)

    k_in = [pltpu.make_async_copy(k_hbm.at[:, columns(h)], packs.at[0, h, pl.ds(0, BLOCK)], k_sem.at[h]) for h in range(KV)]
    v_in = [pltpu.make_async_copy(v_hbm.at[:, columns(h)], raw.at[h], v_sem.at[h]) for h in range(KV)]
    wide = GROUP * HEAD
    q_in = [pltpu.make_async_copy(q_hbm.at[:, pl.ds(g * wide, wide)], q.at[g], q_sem.at[g]) for g in range(KV)]
    for copy in v_in + k_in + q_in:
        copy.start()

    seg = seg_ref[...].astype(F32)
    lower = lax.broadcasted_iota(jnp.int32, (16, HEAD), 0) < 8
    own_rows = jnp.where(lower, seg[:, :HEAD], seg[:, HEAD:]).astype(BF16)
    flips = (1 - 2 * signs_ref[...]).astype(F32)
    table = hadamard_signs()

    for place, comes in ((1, has_near), (2, has_hop), (3, has_far)):
        @pl.when(jnp.logical_not(comes))
        def _():
            for h in range(KV):
                packs[place, h, : 2 * BLOCK, :] = jnp.zeros((2 * BLOCK, HEAD), BF16)
                packs[place, h, 2 * BLOCK :, :] = jnp.full((16, HEAD), NO_DOC, BF16)

    def carry(source, place, h, index, sent):
        return pltpu.make_async_remote_copy(
            src_ref=packs.at[source, h], dst_ref=packs.at[place, h],
            send_sem=send.at[sent, h], recv_sem=recv.at[place - 1, h],
            device_id=device(index), device_id_type=MESH,
        )

    near = [carry(0, 1, h, me + 1, 0) for h in range(KV)]
    hop = [carry(0, 2, h, hop_index, 1) for h in range(KV)]
    far = [carry(1, 3, h, me + n_inner, 2) for h in range(KV)]
    back = [carry(2, 1, h, back_index, 3) for h in range(KV)]
    side = [carry(2, 3, h, me + 1, 3) for h in range(KV)]

    peers = to_near.astype(jnp.int32) + to_hop.astype(jnp.int32) + to_back.astype(jnp.int32)
    def all_here():
        for number in (1, 2, 3):
            @pl.when(peers == number)
            def _():
                pl.semaphore_wait(barrier, number)

    last = inner == n_inner - 1
    first_near = odd | last
    paced_near = jnp.logical_not(first_near | turn)
    for h in range(KV):
        v_in[h].wait()
        turned = jnp.dot((raw[h].astype(F32) * flips).astype(BF16), table, preferred_element_type=F32)
        packs[0, h, BLOCK : 2 * BLOCK, :] = (turned * F32(1 / math.sqrt(HEAD))).astype(BF16)
        packs[0, h, 2 * BLOCK :, :] = own_rows
        k_in[h].wait()
        if h == 0:
            all_here()
        pl.when(to_near & first_near)(near[h].start)
        pl.when(to_hop)(hop[h].start)

    own = documents(packs[0, 0, 2 * BLOCK :, :])
    same = lax.dot_general(own.astype(BF16), own.astype(BF16), ROW_BY_ROW, preferred_element_type=F32)
    row = lax.broadcasted_iota(jnp.int32, (BLOCK, BLOCK), 0)
    column = lax.broadcasted_iota(jnp.int32, (BLOCK, BLOCK), 1)
    bias[...] = jnp.where((same > 0.5) & (row >= column), F32(0), F32(NEG))
    away[...] = jnp.where(own > 0.5, F32(0), F32(NEG)).astype(BF16)
    ones = jnp.ones((BLOCK, HEAD), BF16)

    def values_of(place, g):
        return jnp.concatenate([packs[place, g, BLOCK : 2 * BLOCK, :], ones], axis=1)

    def keys_of(place, g):
        return jnp.concatenate([packs[place, g, :BLOCK, :], docs[place - 1]], axis=1)

    def query_of(g, j):
        return q[g, :, j * HEAD : (j + 1) * HEAD]

    def read_documents(place, exists):
        found = documents(packs[place, 0, 2 * BLOCK :, :])
        none = (lax.broadcasted_iota(jnp.int32, (BLOCK, HEAD), 1) == NO_DOC).astype(F32)
        docs[place - 1] = jnp.where(exists, found, none).astype(BF16)

    def begin(g):
        q_in[g].wait()
        pl.when(to_near & paced_near)(near[g].start)
        pl.when(has_hop)(hop[g].wait_recv)
        pl.when(to_back)(back[g].start)
        pl.when(to_near & even & turn)(near[g].start)
        pl.when(to_side_first if g < KV // 2 else to_side)(side[g].start)
        if g == 0:
            read_documents(2, me >= n_inner)
        for j in range(GROUP):
            query = query_of(g, j)
            wide_query = jnp.concatenate([query, away[...]], axis=1)
            own_scores = lax.dot_general(query, packs[0, g, :BLOCK, :], ROW_BY_ROW, preferred_element_type=F32) + bias[...]
            hop_scores = lax.dot_general(wide_query, keys_of(2, g), ROW_BY_ROW, preferred_element_type=F32)
            peak = row_peak(own_scores, hop_scores)
            total = None
            for place, scores in ((0, own_scores), (2, hop_scores)):
                weights = jnp.exp2((scores - twice(peak)) * SCALE).astype(BF16)
                part = jnp.dot(weights, values_of(place, g), preferred_element_type=F32)
                total = part if total is None else total + part
            top[g * GROUP + j] = peak
            acc[g * GROUP + j] = total

    def arrive(h, here):
        pl.when(has_near & here)(near[h].wait_recv)
        pl.when((to_far_first if h < KV // 2 else to_far_late) & here)(far[h].start)

    def merged(place, g, j):
        query = jnp.concatenate([query_of(g, j), away[...]], axis=1)
        scores = lax.dot_general(query, keys_of(place, g), ROW_BY_ROW, preferred_element_type=F32)
        before = top[g * GROUP + j]
        peak = jnp.maximum(row_peak(scores, scores), before)
        weights = jnp.exp2((scores - twice(peak)) * SCALE).astype(BF16)
        part = jnp.dot(weights, values_of(place, g), preferred_element_type=F32)
        return acc[g * GROUP + j] * twice(jnp.exp2((before - peak) * SCALE)) + part, peak

    def extend(g):
        if g == 0:
            read_documents(1, me >= 1)
        for j in range(GROUP):
            acc[g * GROUP + j], top[g * GROUP + j] = merged(1, g, j)

    def finish(g):
        pl.when(has_far)(far[g].wait_recv)
        if g == 0:
            read_documents(3, me >= n_inner + 1)
        for j in range(GROUP):
            total, _ = merged(3, g, j)
            mass = total[:, HEAD:]
            share = pl.reciprocal(mass, approx=True)
            share = share * (2 - mass * share)
            out[:, (g * GROUP + j) * HEAD : (g * GROUP + j + 1) * HEAD] = (total[:, :HEAD] * share).astype(BF16)

    early_near = even & last
    later = jnp.logical_not(early_near)
    for g in range(KV):
        begin(g)
        arrive(g, early_near)
    arrive(0, later)
    extend(0)
    arrive(1, later)
    finish(0)
    extend(1)
    arrive(2, later)
    finish(1)
    extend(2)
    arrive(3, later)
    finish(2)
    extend(3)
    finish(3)
    for h in range(KV):
        pl.when(to_near)(near[h].wait_send)
        pl.when(to_hop)(hop[h].wait_send)
        pl.when(to_far_first if h < KV // 2 else to_far_late)(far[h].wait_send)
        pl.when(to_back)(back[h].wait_send)
        pl.when(to_side_first if h < KV // 2 else to_side)(side[h].wait_send)


def solution(mesh):
    n_outer, n_inner = mesh.shape["outer"], mesh.shape["inner"]

    def on_device(queries, keys, values, segment, signs):
        anywhere = pl.BlockSpec(memory_space=pl.ANY)
        here = pl.BlockSpec(memory_space=pltpu.VMEM)
        return pl.pallas_call(
            functools.partial(kernel, n_outer, n_inner),
            out_shape=pltpu.VMEM(queries.shape, BF16),
            in_specs=[anywhere, anywhere, anywhere, here, here],
            out_specs=here,
            scratch_shapes=[
                pltpu.VMEM((KV, BLOCK, GROUP * HEAD), BF16),
                pltpu.VMEM((KV, BLOCK, HEAD), BF16),
                pltpu.VMEM((4, KV, ROWS, HEAD), BF16),
                pltpu.VMEM((KV * GROUP, BLOCK, HEAD), F32),
                pltpu.VMEM((KV * GROUP, BLOCK, 2 * HEAD), F32),
                pltpu.VMEM((BLOCK, BLOCK), F32),
                pltpu.VMEM((BLOCK, HEAD), BF16),
                pltpu.VMEM((3, BLOCK, HEAD), BF16),
                pltpu.SemaphoreType.DMA((KV,)),
                pltpu.SemaphoreType.DMA((KV,)),
                pltpu.SemaphoreType.DMA((KV,)),
                pltpu.SemaphoreType.DMA((4, KV)),
                pltpu.SemaphoreType.DMA((3, KV)),
            ],
            compiler_params=pltpu.CompilerParams(
                collective_id=0, has_side_effects=True, vmem_limit_bytes=60 * 2**20
            ),
        )(queries, keys, values, segment.reshape(1, BLOCK), signs.reshape(1, HEAD))

    placed = (
        P(("outer", "inner"), None),
        P(("outer", "inner"), None),
        P(("outer", "inner"), None),
        P(("outer", "inner")),
        P(),
    )
    return jax.shard_map(
        on_device, mesh=mesh, in_specs=placed, out_specs=P(("outer", "inner"), None), check_vma=False
    )
```

```python
import functools
import math

import jax
import jax.numpy as jnp
from jax import lax
from jax.experimental import pallas as pl
from jax.experimental.pallas import tpu as pltpu
from jax.sharding import PartitionSpec as P

MESH = pl.DeviceIdType.MESH
BLOCK = 256
HEAD = 128
KV = 4
GROUP = 8
ROWS = 2 * BLOCK + 16
NEG = -1e30
NO_DOC = 127
SCALE = math.log2(math.e) / math.sqrt(HEAD)
ROW_BY_ROW = (((1,), (1,)), ((), ()))
BF16 = jnp.bfloat16
F32 = jnp.float32


def hadamard_signs():
    left = lax.broadcasted_iota(jnp.int32, (HEAD, HEAD), 0)
    right = lax.broadcasted_iota(jnp.int32, (HEAD, HEAD), 1)
    both = left & right
    both = both ^ (both >> 4)
    both = both ^ (both >> 2)
    both = both ^ (both >> 1)
    return (1 - 2 * (both & 1)).astype(F32).astype(BF16)


def documents(packet_rows):
    parts = []
    for half in range(2):
        row = packet_rows[8 * half : 8 * half + 1, :].astype(F32)
        ids = lax.broadcasted_iota(jnp.int32, (HEAD, HEAD), 0).astype(F32)
        parts.append(jnp.where(row == ids, F32(1), F32(0)).T)
    return jnp.concatenate(parts, axis=0)


def twice(block):
    return jnp.concatenate([block, block], axis=1)


def row_peak(first, second):
    both = jnp.maximum(first, second)
    both = jnp.maximum(both[:, :HEAD], both[:, HEAD:])
    return jnp.broadcast_to(jnp.max(both, axis=1, keepdims=True), (BLOCK, HEAD))


def kernel(
    n_outer, n_inner, q_hbm, k_hbm, v_hbm, seg_ref, signs_ref, out,
    q, raw, packs, top, acc, bias, away, docs,
    q_sem, k_sem, v_sem, send, recv,
):
    count = n_outer * n_inner

    def device(index):
        return {"outer": lax.div(index, n_inner), "inner": lax.rem(index, n_inner)}

    outer, inner = lax.axis_index("outer"), lax.axis_index("inner")
    me = outer * n_inner + inner
    even = lax.rem(outer, 2) == 0
    odd = lax.rem(outer, 2) == 1
    low = lax.rem(lax.div(outer, 2), 2)
    half = n_inner // 2
    turn = inner == half - 1
    wraps = odd & turn
    late = (inner == half - 1) | (inner == n_inner - 1)
    early = (inner == half - 2) | (inner == n_inner - 2)

    has_near = me >= 1
    has_hop = (me >= n_inner) | (me == half - 1)
    has_far = me >= n_inner + 1
    to_near = (me + 1 < count) & jnp.logical_not(wraps)
    to_hop = (me + n_inner < count) | (me == count - half - 1)
    to_back = even & turn
    to_far = has_near & (me + n_inner < count)
    to_far_late = to_far & jnp.logical_not(odd & late)
    to_side = even & early & (me >= n_inner)
    to_side_first = to_side & (inner == half - 2)
    to_side_last = to_side | (even & turn & (low == 0) & (me >= n_inner))
    to_far_last = to_far_late & jnp.logical_not(odd & (inner == half) & (low == 1))
    to_far_first = to_far & jnp.logical_not(odd & turn)

    hop_index = lax.rem(me + n_inner, count)
    back_index = lax.rem(me - n_inner + 1 + count, count)
    hop_source = lax.rem(me - n_inner + count, count)
    near_source = jnp.where(odd & (inner == half), lax.rem(me + n_inner - 1, count), me - 1)

    barrier = pltpu.get_barrier_semaphore()
    for comes, source in ((has_near, near_source), (has_hop, hop_source)):
        @pl.when(comes)
        def _():
            pl.semaphore_signal(barrier, inc=1, device_id=device(source), device_id_type=MESH)

    def columns(h):
        return pl.ds(h * HEAD, HEAD)

    k_in = [pltpu.make_async_copy(k_hbm.at[:, columns(h)], packs.at[0, h, pl.ds(0, BLOCK)], k_sem.at[h]) for h in range(KV)]
    v_in = [pltpu.make_async_copy(v_hbm.at[:, columns(h)], raw.at[h], v_sem.at[h]) for h in range(KV)]
    wide = GROUP * HEAD
    q_in = [pltpu.make_async_copy(q_hbm.at[:, pl.ds(g * wide, wide)], q.at[g], q_sem.at[g]) for g in range(KV)]
    for copy in v_in + k_in + q_in:
        copy.start()

    seg = seg_ref[...].astype(F32)
    lower = lax.broadcasted_iota(jnp.int32, (16, HEAD), 0) < 8
    own_rows = jnp.where(lower, seg[:, :HEAD], seg[:, HEAD:]).astype(BF16)
    flips = (1 - 2 * signs_ref[...]).astype(F32)
    table = hadamard_signs()

    for place, comes in ((1, has_near), (2, has_hop), (3, has_far)):
        @pl.when(jnp.logical_not(comes))
        def _():
            for h in range(KV):
                packs[place, h, : 2 * BLOCK, :] = jnp.zeros((2 * BLOCK, HEAD), BF16)
                packs[place, h, 2 * BLOCK :, :] = jnp.full((16, HEAD), NO_DOC, BF16)

    def carry(source, place, h, index, sent):
        return pltpu.make_async_remote_copy(
            src_ref=packs.at[source, h], dst_ref=packs.at[place, h],
            send_sem=send.at[sent, h], recv_sem=recv.at[place - 1, h],
            device_id=device(index), device_id_type=MESH,
        )

    near = [carry(0, 1, h, me + 1, 0) for h in range(KV)]
    hop = [carry(0, 2, h, hop_index, 1) for h in range(KV)]
    far = [carry(1, 3, h, me + n_inner, 2) for h in range(KV)]
    back = [carry(2, 1, h, back_index, 3) for h in range(KV)]
    side = [carry(2, 3, h, me + 1, 4) for h in range(KV)]

    peers = to_near.astype(jnp.int32) + to_hop.astype(jnp.int32) + to_back.astype(jnp.int32)
    def all_here():
        for number in (1, 2, 3):
            @pl.when(peers == number)
            def _():
                pl.semaphore_wait(barrier, number)

    last = inner == n_inner - 1
    first_near = odd | last
    paced_near = jnp.logical_not(first_near | turn)
    for h in range(KV):
        v_in[h].wait()
        turned = jnp.dot((raw[h].astype(F32) * flips).astype(BF16), table, preferred_element_type=F32)
        packs[0, h, BLOCK : 2 * BLOCK, :] = (turned * F32(1 / math.sqrt(HEAD))).astype(BF16)
        packs[0, h, 2 * BLOCK :, :] = own_rows
        k_in[h].wait()
        if h == 0:
            all_here()
        pl.when(to_near & first_near)(near[h].start)
        pl.when(to_hop)(hop[h].start)

    own = documents(packs[0, 0, 2 * BLOCK :, :])
    same = lax.dot_general(own.astype(BF16), own.astype(BF16), ROW_BY_ROW, preferred_element_type=F32)
    row = lax.broadcasted_iota(jnp.int32, (BLOCK, BLOCK), 0)
    column = lax.broadcasted_iota(jnp.int32, (BLOCK, BLOCK), 1)
    bias[...] = jnp.where((same > 0.5) & (row >= column), F32(0), F32(NEG))
    away[...] = jnp.where(own > 0.5, F32(0), F32(NEG)).astype(BF16)
    ones = jnp.ones((BLOCK, HEAD), BF16)

    def values_of(place, g):
        return jnp.concatenate([packs[place, g, BLOCK : 2 * BLOCK, :], ones], axis=1)

    def keys_of(place, g):
        return jnp.concatenate([packs[place, g, :BLOCK, :], docs[place - 1]], axis=1)

    def query_of(g, j):
        return q[g, :, j * HEAD : (j + 1) * HEAD]

    def read_documents(place, exists):
        found = documents(packs[place, 0, 2 * BLOCK :, :])
        none = (lax.broadcasted_iota(jnp.int32, (BLOCK, HEAD), 1) == NO_DOC).astype(F32)
        docs[place - 1] = jnp.where(exists, found, none).astype(BF16)

    def begin(g):
        q_in[g].wait()
        pl.when(to_near & paced_near)(near[g].start)
        pl.when(has_hop)(hop[g].wait_recv)
        pl.when(to_back)(back[g].start)
        pl.when(to_near & even & turn)(near[g].start)
        pl.when((to_side_first, to_side_first, to_side, to_side_last)[g])(side[g].start)
        if g == 0:
            read_documents(2, me >= n_inner)
        for j in range(GROUP):
            query = query_of(g, j)
            wide_query = jnp.concatenate([query, away[...]], axis=1)
            own_scores = lax.dot_general(query, packs[0, g, :BLOCK, :], ROW_BY_ROW, preferred_element_type=F32) + bias[...]
            hop_scores = lax.dot_general(wide_query, keys_of(2, g), ROW_BY_ROW, preferred_element_type=F32)
            peak = row_peak(own_scores, hop_scores)
            total = None
            for place, scores in ((0, own_scores), (2, hop_scores)):
                weights = jnp.exp2((scores - twice(peak)) * SCALE).astype(BF16)
                part = jnp.dot(weights, values_of(place, g), preferred_element_type=F32)
                total = part if total is None else total + part
            top[g * GROUP + j] = peak
            acc[g * GROUP + j] = total

    def arrive(h, here):
        pl.when(has_near & here)(near[h].wait_recv)
        pl.when((to_far_first, to_far_first, to_far_late, to_far_last)[h] & here)(far[h].start)

    def merged(place, g, j):
        query = jnp.concatenate([query_of(g, j), away[...]], axis=1)
        scores = lax.dot_general(query, keys_of(place, g), ROW_BY_ROW, preferred_element_type=F32)
        before = top[g * GROUP + j]
        peak = jnp.maximum(row_peak(scores, scores), before)
        weights = jnp.exp2((scores - twice(peak)) * SCALE).astype(BF16)
        part = jnp.dot(weights, values_of(place, g), preferred_element_type=F32)
        return acc[g * GROUP + j] * twice(jnp.exp2((before - peak) * SCALE)) + part, peak

    def extend(g):
        if g == 0:
            read_documents(1, me >= 1)
        for j in range(GROUP):
            acc[g * GROUP + j], top[g * GROUP + j] = merged(1, g, j)

    def finish(g):
        pl.when(has_far)(far[g].wait_recv)
        if g == 0:
            read_documents(3, me >= n_inner + 1)
        for j in range(GROUP):
            total, _ = merged(3, g, j)
            mass = total[:, HEAD:]
            share = pl.reciprocal(mass, approx=True)
            share = share * (2 - mass * share)
            out[:, (g * GROUP + j) * HEAD : (g * GROUP + j + 1) * HEAD] = (total[:, :HEAD] * share).astype(BF16)

    early_near = even & last
    later = jnp.logical_not(early_near)
    for g in range(KV):
        begin(g)
        arrive(g, early_near)
    arrive(0, later)
    extend(0)
    arrive(1, later)
    finish(0)
    extend(1)
    arrive(2, later)
    finish(1)
    extend(2)
    arrive(3, later)
    finish(2)
    extend(3)
    finish(3)
    for h in range(KV):
        pl.when(to_near)(near[h].wait_send)
        pl.when(to_hop)(hop[h].wait_send)
        pl.when((to_far_first, to_far_first, to_far_late, to_far_last)[h])(far[h].wait_send)
        pl.when(to_back)(back[h].wait_send)
        pl.when((to_side_first, to_side_first, to_side, to_side_last)[h])(side[h].wait_send)


def solution(mesh):
    n_outer, n_inner = mesh.shape["outer"], mesh.shape["inner"]

    def on_device(queries, keys, values, segment, signs):
        anywhere = pl.BlockSpec(memory_space=pl.ANY)
        here = pl.BlockSpec(memory_space=pltpu.VMEM)
        return pl.pallas_call(
            functools.partial(kernel, n_outer, n_inner),
            out_shape=pltpu.VMEM(queries.shape, BF16),
            in_specs=[anywhere, anywhere, anywhere, here, here],
            out_specs=here,
            scratch_shapes=[
                pltpu.VMEM((KV, BLOCK, GROUP * HEAD), BF16),
                pltpu.VMEM((KV, BLOCK, HEAD), BF16),
                pltpu.VMEM((4, KV, ROWS, HEAD), BF16),
                pltpu.VMEM((KV * GROUP, BLOCK, HEAD), F32),
                pltpu.VMEM((KV * GROUP, BLOCK, 2 * HEAD), F32),
                pltpu.VMEM((BLOCK, BLOCK), F32),
                pltpu.VMEM((BLOCK, HEAD), BF16),
                pltpu.VMEM((3, BLOCK, HEAD), BF16),
                pltpu.SemaphoreType.DMA((KV,)),
                pltpu.SemaphoreType.DMA((KV,)),
                pltpu.SemaphoreType.DMA((KV,)),
                pltpu.SemaphoreType.DMA((5, KV)),
                pltpu.SemaphoreType.DMA((3, KV)),
            ],
            compiler_params=pltpu.CompilerParams(
                collective_id=0, has_side_effects=True, vmem_limit_bytes=60 * 2**20
            ),
        )(queries, keys, values, segment.reshape(1, BLOCK), signs.reshape(1, HEAD))

    placed = (
        P(("outer", "inner"), None),
        P(("outer", "inner"), None),
        P(("outer", "inner"), None),
        P(("outer", "inner")),
        P(),
    )
    return jax.shard_map(
        on_device, mesh=mesh, in_specs=placed, out_specs=P(("outer", "inner"), None), check_vma=False
    )
```
